32 devices in a mesh: group: 16 (over z, y, x), depth: 2 (over core).
Axes of the slice: x: 2, y: 2, z: 4, core: 2. Of those that a mesh axis runs over, the one named last changes fastest.
Arguments:
- fwd_now: float32 [125, 8192], P(None, ('group', 'depth')), may hold values from -6 to 6
- fwd_prev: float32 [125, 8192], P(None, ('group', 'depth')), may hold values from -6 to 6
- adj_now: float32 [125, 8192], P(None, ('group', 'depth')), may hold values from -6 to 6
- adj_prev: float32 [125, 8192], P(None, ('group', 'depth')), may hold values from -6 to 6
- speed_sq: float32 [8192], P(('group', 'depth')), may hold values from 0.5 to 2
- face_lists: int32 [6, 8192], P(None, ('group', 'depth')), may hold values from 0 to 511, as said below
- send_low: int32 [8192], P(('group', 'depth')), may hold values from 0 to 255, as said below
- send_high: int32 [8192], P(('group', 'depth')), may hold values from 0 to 255, as said below
- send_radial: int32 [512], P(('group', 'depth')), may hold values from 0 to 255, as said below
- owner_dev: int32 [8192, 1], P(('group', 'depth')), may hold values from 0 to 31; in each aligned block of 256 rows (0 to 255, 256 to 511, ...) at most 14 rows name the same one
- param_slot: int32 [8192], P(('group', 'depth')), may hold values from 0 to 127
Outputs:
- fwd_out: float32 [125, 8192], P(None, ('group', 'depth'))
- adj_out: float32 [125, 8192], P(None, ('group', 'depth'))
- param_grad: float32 [4096, 125], P(('group', 'depth'))
The draws below stay inside these ranges and needn't reach their ends.
Inputs may be any that keep to these rules, and one draw needn't show every extreme that they name: Each device's elements form a structured block of 1 x 16 x 16 elements stored in a device-specific order; face_lists names each element's touching face in its direction's pool, or the pool's last zero entry at an outer surface or a side of the block along the second lateral direction. `send_low`: distinct elements of one device, ordered by position on the face. `send_high`: distinct elements of one device, ordered by position on the face. `send_radial`: distinct elements of one device: the top layer on depth 0, the bottom layer on depth 1. `owner_dev`: among the elements of one device, no owner is named more than 14 times.
All inputs are finite; a program needn't handle non-finite values.
Results may differ from the reference program's by a relative error of at most 0.0001.
Values sent between devices are 32-bit elements; how exact they have to be, the bound alone decides.
A program may use at most 64 MiB of HBM per device.

```python
import math
import jax
import jax.numpy as jnp
import numpy as np
from jax import lax

NODES = 125
STEPS = 4
GA = 1
GB = 16
GC = 16
P_DEV = 128
E_DEV = 256
E_TOTAL = 8192
P_TOTAL = 4096
CAP = 14
N_GROUP = 16
N_DEPTH = 2


def storage_order(key):
    devices = N_GROUP * N_DEPTH
    base = jax.random.fold_in(key, 7)
    return jax.vmap(lambda i: jax.random.permutation(jax.random.fold_in(base, i), E_DEV))(jnp.arange(devices)).astype(jnp.int32)


def draw_send_low(key, part):
    order = storage_order(key)
    return order[:, jnp.arange(GB * GC)].reshape(-1).astype(jnp.int32)


def draw_send_high(key, part):
    order = storage_order(key)
    return order[:, (GA - 1) * GB * GC + jnp.arange(GB * GC)].reshape(-1).astype(jnp.int32)


def draw_send_radial(key, part):
    order = storage_order(key)
    devices = N_GROUP * N_DEPTH
    places = jnp.arange(GA * GB)
    depth_here = (jnp.arange(devices) % N_DEPTH)[:, None]
    top_layer = order[:, places * GC + GC - 1]
    bottom_layer = order[:, places * GC]
    return jnp.where(depth_here == 0, top_layer, bottom_layer).reshape(-1).astype(jnp.int32)


def draw_face_lists(key, part):
    order = storage_order(key)
    devices = N_GROUP * N_DEPTH
    logical = jnp.arange(E_DEV)
    along_a = logical // (GB * GC)
    along_b = logical // GC % GB
    along_g = logical % GC
    depth_here = (jnp.arange(devices) % N_DEPTH)[:, None]

    def moved(offset):
        return jnp.take(order, jnp.clip(logical + offset, 0, E_DEV - 1), axis=1)
    lateral_slot = E_DEV + along_b * GC + along_g
    radial_slot = E_DEV + along_a * GB + along_b
    radial_zero = E_DEV + GA * GB
    first = jnp.where(along_a > 0, moved(-GB * GC), lateral_slot)
    second = jnp.where(along_a < GA - 1, moved(GB * GC), lateral_slot)
    third = jnp.where(along_b > 0, moved(-GC), E_DEV)
    fourth = jnp.where(along_b < GB - 1, moved(GC), E_DEV)
    fifth = jnp.where(along_g > 0, moved(-1), jnp.where(depth_here == 1, radial_slot, radial_zero))
    sixth = jnp.where(along_g < GC - 1, moved(1), jnp.where(depth_here == 0, radial_slot, radial_zero))
    values = jnp.stack([jnp.broadcast_to(v, (devices, E_DEV)) for v in [first, second, third, fourth, fifth, sixth]], axis=1).astype(jnp.int32)
    device_ids = jnp.arange(devices)[:, None, None]
    direction_ids = jnp.arange(6)[None, :, None]
    placed = jnp.zeros((devices, 6, E_DEV), jnp.int32).at[device_ids, direction_ids, order[:, None, :]].set(values)
    return placed.transpose(1, 0, 2).reshape(6, devices * E_DEV).astype(jnp.int32)


def set_ends(values, stream_key, low, largest):
    extent = values.shape
    index_at = [jax.random.randint(jax.random.fold_in(stream_key, axis), (), 0, extent[axis]) for axis in range(len(extent))]
    values = values.at[tuple(index_at)].set(low)
    longest = extent.index(max(extent))
    index_at[longest] = (index_at[longest] + 1) % extent[longest]
    return values.at[tuple(index_at)].set(largest)


def block_scale(own_key, shape, cuts, smallest, high):
    def one(dim, shards_of):
        steps = jax.random.uniform(jax.random.fold_in(jax.random.fold_in(own_key, 6), dim), (shards_of,), jnp.float32, smallest / len(cuts), high / len(cuts))
        return jnp.repeat(jnp.exp(steps), shape[dim] // shards_of).reshape((-1,) + (1,) * (len(shape) - dim - 1))

    factor_of = one(*cuts[0])
    for cut in cuts[1:]:
        factor_of = factor_of * one(*cut)
    return factor_of


def assign_block(own_key, own, number, rows, amount, top, bound, lean):
    ranking = jax.random.permutation(own_key, amount)
    packed, usual = portions_of(amount, rows * top, bound, lean, True), portions_of(amount, rows * top, bound, lean, False)
    places = jnp.arange(amount)

    def named(lengths, offset_by):
        used = int((lengths > 0).sum())
        fixed = max(1, used // 4)
        passed = fixed + (places - fixed + offset_by * (used - fixed)) % max(1, amount - fixed)
        return jnp.zeros((amount,), jnp.int32).at[ranking[jnp.where(places < fixed, places, passed)]].set(jnp.asarray(lengths, jnp.int32))

    lengths = jnp.where(number % 4 == 0, named(packed, number // 4), named(usual, number - number // 4 - 1))
    mixed = jax.random.permutation(jax.random.fold_in(own, 3), amount)
    donor, taker = mixed[0:amount // 2 * 2:2], mixed[1:amount // 2 * 2:2]
    slack = jnp.minimum(lengths[donor] - 1, bound - lengths[taker]) // 2
    slack = jnp.where((donor == ranking[0]) | (taker == ranking[0]) | (lengths[taker] == 0), 0, jnp.maximum(slack, 0))
    passed = jax.random.randint(jax.random.fold_in(own, 4), (amount // 2,), 0, 1 << 20) % (slack + 1)
    lengths = lengths.at[donor].add(-passed).at[taker].add(passed)
    labels = jnp.searchsorted(jnp.cumsum(lengths), jnp.arange(rows * top), side="right").astype(jnp.int32)
    table = labels.reshape(top, rows).T
    table = table[jax.random.permutation(jax.random.fold_in(own, 1), rows)]
    offset_by = jax.random.randint(jax.random.fold_in(own, 2), (rows, 1), 0, top)
    return jnp.take_along_axis(table, (jnp.arange(top)[None, :] + offset_by) % top, axis=1)


def portions_of(number_of, total, limit, slope, full):
    weights = [(1 << 20) // math.isqrt(grade ** slope) + 1 for grade in range(1, number_of + 1)]
    largest = limit if full else min(limit, max(-(-total // number_of), total * weights[0] // sum(weights)))
    least = 1 if total - largest >= number_of - 1 else 0
    counts, rest = [largest] + [least] * (number_of - 1), total - largest - least * (number_of - 1)
    while rest > 0:
        movable = [i for i in range(1, number_of) if counts[i] < largest] or [i for i in range(1, number_of) if counts[i] < limit]
        mass, budget = sum([weights[i] for i in movable]), rest
        for i in movable:
            more = min(limit - counts[i], max(1, budget * weights[i] // mass), rest)
            counts[i] = counts[i] + more
            rest = rest - more
    return np.array(counts)


def noise(stream_key, shape, scale, limit, pieces=(), held_as=jnp.bfloat16):
    values = scale * jax.random.normal(stream_key, shape, jnp.float32)
    if pieces:
        values = values * block_scale(stream_key, shape, pieces, -0.22, 0.18)
    return jnp.clip(values, -limit, limit).astype(held_as)


def setup_inputs(seed: int = 0) -> dict:
    arg_keys = jax.random.split(jax.random.key(seed), 12)
    fwd_now = noise(arg_keys[0], (NODES, E_TOTAL), 1.0, 6.0, ((1, 32),), jnp.float32)
    fwd_prev = noise(arg_keys[1], (NODES, E_TOTAL), 1.0, 6.0, ((1, 32),), jnp.float32)
    adj_now = noise(arg_keys[2], (NODES, E_TOTAL), 1.0, 6.0, ((1, 32),), jnp.float32)
    adj_prev = noise(arg_keys[3], (NODES, E_TOTAL), 1.0, 6.0, ((1, 32),), jnp.float32)
    speed_sq = jnp.clip(jnp.exp(math.log(2.0) - 1.3862944 * jax.random.uniform(arg_keys[4], (E_TOTAL,), jnp.float32) ** block_scale(arg_keys[4], (E_TOTAL,), ((0, 32),), -0.2, 0.2)), 0.5, 2.0)
    face_lists = draw_face_lists(jax.random.fold_in(arg_keys[11], 71), 0)
    send_low = draw_send_low(jax.random.fold_in(arg_keys[11], 71), 0)
    send_high = draw_send_high(jax.random.fold_in(arg_keys[11], 71), 0)
    send_radial = draw_send_radial(jax.random.fold_in(arg_keys[11], 71), 0)
    owner_dev_keys = jax.random.split(jax.random.fold_in(arg_keys[9], 1), E_TOTAL // E_DEV)
    owner_dev_turns = jax.random.permutation(jax.random.fold_in(arg_keys[9], 3), E_TOTAL // E_DEV)
    owner_dev = jax.vmap(lambda own, number: assign_block(jax.random.fold_in(arg_keys[9], 2), own, number, E_DEV, N_GROUP * N_DEPTH, 1, CAP, 2))(owner_dev_keys, owner_dev_turns).reshape((E_TOTAL, 1))
    param_slot = set_ends(jax.random.randint(arg_keys[10], (E_TOTAL,), 0, P_DEV), jax.random.fold_in(arg_keys[10], 1), 0, P_DEV - 1).astype(jnp.int32)
    return dict(fwd_now=fwd_now, fwd_prev=fwd_prev, adj_now=adj_now, adj_prev=adj_prev, speed_sq=speed_sq, face_lists=face_lists, send_low=send_low, send_high=send_high, send_radial=send_radial, owner_dev=owner_dev, param_slot=param_slot)


PENALTY = 40.0
DT_SQUARED = 0.001
KERNEL_SCALE = 0.05

def gll_tables():
    points = np.array([-1.0, -math.sqrt(3.0 / 7.0), 0.0, math.sqrt(3.0 / 7.0), 1.0])
    weights = np.array([0.1, 49.0 / 90.0, 32.0 / 45.0, 49.0 / 90.0, 0.1])
    barycentric = np.array([np.prod([points[i] - points[m] for m in range(5) if m != i]) for i in range(5)])
    derivative = np.zeros((5, 5))
    for i in range(5):
        for j in range(5):
            if i != j:
                derivative[i, j] = barycentric[i] / (barycentric[j] * (points[i] - points[j]))
            else:
                derivative[i, j] = sum((1.0 / (points[i] - points[m]) for m in range(5) if m != i))
    return (weights, derivative)

def apply_axis(table, field, axis):
    forms = ['pi,i...->p...', 'pj,ij...->ip...', 'pk,ijk...->ijp...']
    return jnp.einsum(forms[axis], table, field, precision=lax.Precision.HIGHEST)

def face_index(direction):
    whole = slice(None)
    spots = [(0,), (4,), (whole, 0), (whole, 4), (whole, whole, 0), (whole, whole, 4)]
    return spots[direction]

def faces_of(field):
    return [field[face_index(f)].reshape((25,) + field.shape[3:]) for f in range(6)]

def weight_cube(ndim):
    weights, derivative = gll_tables()
    cube = weights.reshape(5, 1, 1) * weights.reshape(1, 5, 1) * weights.reshape(1, 1, 5)
    return jnp.asarray(cube.reshape((5, 5, 5) + (1,) * (ndim - 3)), jnp.float32)

def weight_face(ndim):
    weights, derivative = gll_tables()
    square = weights.reshape(5, 1) * weights.reshape(1, 5)
    return jnp.asarray(square.reshape((5, 5) + (1,) * (ndim - 3)), jnp.float32)

def accelerate(field, grads, coef, neighbours):
    weights, derivative = gll_tables()
    table_t = jnp.asarray(derivative.T, jnp.float32)
    cube = weight_cube(field.ndim)
    stiff = apply_axis(table_t, cube * coef * grads[0], 0)
    stiff = stiff + apply_axis(table_t, cube * coef * grads[1], 1)
    stiff = stiff + apply_axis(table_t, cube * coef * grads[2], 2)
    penal = jnp.zeros_like(field)
    wface = weight_face(field.ndim)
    for f in range(6):
        spot = face_index(f)
        own = field[spot]
        other = neighbours[f].reshape(own.shape)
        penal = penal.at[spot].add(PENALTY * wface * (own - other))
    return -(stiff + penal) / cube

def reference(fwd_now, fwd_prev, adj_now, adj_prev, speed_sq, face_lists, send_low, send_high, send_radial, owner_dev, param_slot):
    weights, derivative = gll_tables()
    table = jnp.asarray(derivative, jnp.float32)
    shape = (5, 5, 5, N_GROUP, N_DEPTH, E_DEV)
    state = jnp.stack([fwd_now.reshape(shape), adj_now.reshape(shape)], axis=3)
    previous = jnp.stack([fwd_prev.reshape(shape), adj_prev.reshape(shape)], axis=3)
    coef = speed_sq.reshape(N_GROUP, N_DEPTH, E_DEV)
    lists = face_lists.reshape(6, N_GROUP, N_DEPTH, E_DEV)
    lows = send_low.reshape(N_GROUP, N_DEPTH, -1)[None, None]
    highs = send_high.reshape(N_GROUP, N_DEPTH, -1)[None, None]
    radials = send_radial.reshape(N_GROUP, N_DEPTH, -1)[None, None]
    depth_here = jnp.arange(N_DEPTH).reshape(1, 1, 1, N_DEPTH, 1)
    kernel_sum = jnp.zeros((5, 5, 5, N_GROUP, N_DEPTH, E_DEV), jnp.float32)
    for step in range(STEPS):
        grads = [apply_axis(table, state, d) for d in range(3)]
        product = grads[0][:, :, :, 0] * grads[0][:, :, :, 1] + grads[1][:, :, :, 0] * grads[1][:, :, :, 1] + grads[2][:, :, :, 0] * grads[2][:, :, :, 1]
        kernel_sum = kernel_sum + KERNEL_SCALE * weight_cube(6) * coef * product
        faces = faces_of(state)
        from_low = jnp.roll(jnp.take_along_axis(faces[1], highs, axis=-1), 1, axis=2)
        from_high = jnp.roll(jnp.take_along_axis(faces[0], lows, axis=-1), -1, axis=2)
        sent_radial = jnp.where(depth_here == 0, jnp.take_along_axis(faces[5], radials, axis=-1), jnp.take_along_axis(faces[4], radials, axis=-1))
        from_radial = sent_radial[:, :, :, ::-1]
        halos = [from_low, from_high, None, None, from_radial, from_radial]
        zero_face = jnp.zeros((25, 2, N_GROUP, N_DEPTH, 1), jnp.float32)
        neighbours = []
        for f in range(6):
            members = [faces[f ^ 1]] + ([halos[f]] if halos[f] is not None else []) + [zero_face]
            pool = jnp.concatenate(members, axis=-1)
            neighbours.append(jnp.take_along_axis(pool, lists[f][None, None], axis=-1))
        accel = accelerate(state, grads, coef, neighbours)
        following = 2.0 * state - previous + DT_SQUARED * accel
        previous = state
        state = following
    fwd_out = state[:, :, :, 0].reshape(NODES, E_TOTAL)
    adj_out = state[:, :, :, 1].reshape(NODES, E_TOTAL)
    cells = owner_dev[:, 0] * P_DEV + param_slot
    blocks = kernel_sum.reshape(NODES, E_TOTAL).T
    param_grad = jax.ops.segment_sum(blocks, cells, num_segments=P_TOTAL)
    return (fwd_out, adj_out, param_grad)
```

```python
import functools
import math

import jax
import jax.numpy as jnp
import numpy as np
from jax import lax
from jax.experimental import pallas as pl
from jax.experimental.pallas import tpu as pltpu
from jax.sharding import PartitionSpec as P

NODES = 125
STEPS = 4
P_DEV = 128
ROWS = 128
FACE = 32

PENALTY = 40.0
DT_SQUARED = 0.001
KERNEL_SCALE = 0.05
MESH = pl.DeviceIdType.MESH
F32, BF16 = jnp.float32, jnp.bfloat16
LOW, HIGH, RADIAL, OWNER, SLOT, TABLE = 6, 7, 8, 9, 10, 16


def gll_tables():
    points = np.array([-1.0, -math.sqrt(3.0 / 7.0), 0.0, math.sqrt(3.0 / 7.0), 1.0])
    weights = np.array([0.1, 49.0 / 90.0, 32.0 / 45.0, 49.0 / 90.0, 0.1])
    barycentric = np.array(
        [np.prod([points[i] - points[m] for m in range(5) if m != i]) for i in range(5)]
    )
    derivative = np.zeros((5, 5))
    for i in range(5):
        for j in range(5):
            if i != j:
                derivative[i, j] = barycentric[i] / (barycentric[j] * (points[i] - points[j]))
            else:
                derivative[i, j] = sum((1.0 / (points[i] - points[m]) for m in range(5) if m != i))
    return (weights, derivative)


def padded(matrix, rows, columns):
    out = np.zeros((rows, columns))
    out[: matrix.shape[0], : matrix.shape[1]] = matrix
    return out


def constants():
    weights, derivative = gll_tables()
    one = np.eye(5)
    grads = [
        np.kron(derivative, np.kron(one, one)),
        np.kron(one, np.kron(derivative, one)),
        np.kron(one, np.kron(one, derivative)),
    ]
    cube = np.kron(weights, np.kron(weights, weights))
    stiff = sum(g.T @ (cube[:, None] * g) for g in grads) / cube[:, None]
    digits = [(n // 25, n // 5 % 5, n % 5) for n in range(NODES)]
    nodes_of = []
    for f in range(6):
        level = 0 if f % 2 == 0 else 4
        nodes_of.append([n for n in range(NODES) if digits[n][f // 2] == level])
    blocks = [padded(m, ROWS, ROWS) for m in grads + [stiff]]
    spread = np.zeros((ROWS, 4 * 2 * FACE))
    for f in range(2, 6):
        pick = np.zeros((FACE, ROWS))
        for a, n in enumerate(nodes_of[f]):
            pick[a, n] = 1.0
            spread[n, (f - 2) * 2 * FACE + a] = 1.0
            spread[n, (f - 2) * 2 * FACE + FACE + a] = 1.0
        blocks.append(pick)
    operator = np.concatenate(blocks, axis=0).astype(np.float32)
    bf = jnp.bfloat16
    high = operator.astype(bf)
    low = (operator - high.astype(np.float32)).astype(bf)
    operator = np.concatenate([high, high, low], axis=1)
    factor = np.zeros((2 * ROWS, 128), np.float32)
    faces = np.array([sum(n in set(nodes_of[f]) for f in range(6)) for n in range(NODES)])
    edge = DT_SQUARED * PENALTY / weights[0]
    factor[:NODES] = (2.0 - edge * faces)[:, None]
    factor[ROWS : ROWS + NODES] = (KERNEL_SCALE * cube)[:, None]
    return operator, spread.astype(bf), factor, edge


def split(values):
    high = values.astype(BF16)
    return high, (values - high.astype(F32)).astype(BF16)


def dot(a, b):
    return jnp.dot(a, b, preferred_element_type=F32)


def onehot(row, count, offset=0):
    places = lax.broadcasted_iota(jnp.int32, (count, row.shape[1]), 0) + offset
    return jnp.where(places == row, 1.0, 0.0).astype(BF16)


def stacked(face, elements):
    high, low = split(face)
    return jnp.concatenate(
        [high[:, :elements], high[:, elements:], low[:, :elements], low[:, elements:]], axis=0
    )


def summed(found):
    total = found[: 2 * FACE] + found[2 * FACE :]
    return jnp.concatenate([total[:FACE], total[FACE:]], axis=1)


def kernel(
    sizes,
    edge,
    fwd_now,
    fwd_prev,
    adj_now,
    adj_prev,
    speed,
    table,
    owner,
    operator,
    spread,
    factor,
    fwd_out,
    adj_out,
    grad_out,
    state,
    previous,
    total,
    picks,
    halo_picks,
    peer_table,
    sent,
    got,
    blocks,
    got_blocks,
    table_send,
    table_recv,
    face_send,
    face_recv,
    block_send,
    block_recv,
):
    groups, layers, elements, capacity, room = sizes
    devices = groups * layers
    both = 2 * elements
    group, layer = lax.axis_index("group"), lax.axis_index("depth")
    me = group * layers + layer
    right = (lax.rem(group + 1, groups), layer)
    left = (lax.rem(group + groups - 1, groups), layer)
    across = (group, 1 - layer)
    partners = (right, left, across)

    barrier = pltpu.get_barrier_semaphore()

    def at(number):
        return (number // layers, lax.rem(number, layers))

    def greet(k, carry):
        other = lax.rem(me + k, devices)
        pl.semaphore_signal(barrier, inc=1, device_id=at(other), device_id_type=MESH)
        return carry

    lax.fori_loop(1, devices, greet, 0)

    state[ROWS - 8 :, :] = jnp.zeros((8, both), F32)
    previous[ROWS - 8 :, :] = jnp.zeros((8, both), F32)
    state[:NODES, :elements] = fwd_now[...]
    state[:NODES, elements:] = adj_now[...]
    previous[:NODES, :elements] = fwd_prev[...]
    previous[:NODES, elements:] = adj_prev[...]
    total[...] = jnp.zeros_like(total)

    def table_copy(side):
        return pltpu.make_async_remote_copy(
            src_ref=table,
            dst_ref=peer_table.at[side],
            send_sem=table_send.at[side],
            recv_sem=table_recv.at[side],
            device_id=partners[side],
            device_id_type=MESH,
        )

    def face_copy(side, step):
        return pltpu.make_async_remote_copy(
            src_ref=sent.at[side, step],
            dst_ref=got.at[side, step],
            send_sem=face_send.at[side, step],
            recv_sem=face_recv.at[side, step],
            device_id=partners[side],
            device_id_type=MESH,
        )

    def block_copy(k):
        other = lax.rem(me + k, devices)
        return pltpu.make_async_remote_copy(
            src_ref=blocks.at[other],
            dst_ref=got_blocks.at[me],
            send_sem=block_send.at[other],
            recv_sem=block_recv.at[me],
            device_id=at(other),
            device_id_type=MESH,
        )

    def block_arrival(k):
        other = lax.rem(me + k, devices)
        return pltpu.make_async_remote_copy(
            src_ref=blocks.at[other],
            dst_ref=got_blocks.at[other],
            send_sem=block_send.at[other],
            recv_sem=block_recv.at[other],
            device_id=at(other),
            device_id_type=MESH,
        )

    rows = lax.broadcasted_iota(jnp.int32, (FACE, both), 0)

    def fill(step):
        top = pltpu.roll(state[ROWS - FACE :, :], FACE - 4, 0)
        sent[0, step] = jnp.where(rows < 25, top, 0.0)
        bottom = pltpu.roll(state[:FACE, :], 4, 0)
        sent[1, step] = jnp.where((rows >= 4) & (rows < 29), bottom, 0.0)
        first = pl.multiple_of(4 * ROWS + 3 * FACE - FACE * layer, FACE)
        high, low = split(state[...])
        pick = operator[pl.ds(first, FACE), : 2 * ROWS]
        sent[2, step] = dot(pick, jnp.concatenate([high, low], axis=0))

    fill(0)
    pl.semaphore_wait(barrier, devices - 1)
    for side in range(3):
        table_copy(side).start()
        face_copy(side, 0).start()

    lists = table[...]
    for f in range(6):
        picks[f] = onehot(lists[f : f + 1], elements)
    before = (owner[...] == lists[OWNER : OWNER + 1]) & (
        lax.broadcasted_iota(jnp.int32, (elements, elements), 0)
        < lax.broadcasted_iota(jnp.int32, (elements, elements), 1)
    )
    position = jnp.sum(jnp.where(before, 1.0, 0.0), axis=0, keepdims=True).astype(jnp.int32)
    placing = lists[OWNER : OWNER + 1] * room + position

    for side in range(3):
        table_copy(side).wait_recv()
    for slot, (side, row, f) in enumerate(
        ((0, HIGH, 0), (1, LOW, 1), (2, RADIAL, 4), (2, RADIAL, 5))
    ):
        theirs = onehot(peer_table[side, row : row + 1], elements)
        mine = onehot(lists[f : f + 1], elements, elements)
        halo_picks[slot] = dot(theirs, mine).astype(BF16)

    speeds = jnp.concatenate([speed[...], speed[...]], axis=1)
    wide = both // 128

    def advance(step, carry):
        high, low = split(state[...])
        parts = dot(operator[...], jnp.concatenate([high, low, high], axis=0))
        product = total[...]
        for d in range(3):
            one = parts[d * ROWS : (d + 1) * ROWS]
            product = product + one[:, :elements] * one[:, elements:]
        total[...] = product

        @pl.when(step == STEPS - 1)
        def _():
            scale = jnp.concatenate([factor[ROWS:]] * (elements // 128), axis=1)
            block = scale * speed[...] * total[...]
            node = lax.broadcasted_iota(jnp.int32, (ROWS, elements), 0)
            label = (lists[SLOT : SLOT + 1] + 1).astype(F32)
            block = jnp.where(node == NODES, label, block)
            block_high, block_low = split(block)
            placer = onehot(placing, devices * room)
            across_nodes = (((1,), (1,)), ((), ()))
            placed = lax.dot_general(placer, block_high, across_nodes, preferred_element_type=F32)
            placed += lax.dot_general(placer, block_low, across_nodes, preferred_element_type=F32)
            blocks[...] = placed.reshape(devices, room, ROWS)

            def start(k, inner):
                block_copy(k).start()
                return inner

            lax.fori_loop(1, devices, start, 0)

        face = [None, None] + [
            stacked(parts[4 * ROWS + f * FACE : 4 * ROWS + (f + 1) * FACE], elements)
            for f in range(4)
        ]
        found = [None, None, dot(face[3], picks[2]), dot(face[2], picks[3])]
        own_low = dot(stacked(sent[0, step], elements), picks[0])
        own_high = dot(stacked(sent[1, step], elements), picks[1])
        face_copy(2, step).wait_recv()
        radial = stacked(got[2, step], elements)
        found.append(dot(face[5], picks[4]) + dot(radial, halo_picks[2]))
        found.append(dot(face[4], picks[5]) + dot(radial, halo_picks[3]))
        pieces = []
        for f in range(2, 6):
            one = found[f].astype(BF16)
            for half in range(2):
                base = 2 * FACE * half
                pieces.append(
                    jnp.concatenate(
                        [one[base : base + FACE], one[base + FACE : base + 2 * FACE]], axis=1
                    )
                )
        penal = dot(spread[...], jnp.concatenate(pieces, axis=0))
        diagonal = jnp.concatenate([factor[:ROWS]] * wide, axis=1)
        now = state[...]
        following = diagonal * now - previous[...]
        following -= DT_SQUARED * speeds * parts[3 * ROWS : 4 * ROWS]
        following += edge * penal
        previous[...] = now
        face_copy(0, step).wait_recv()
        face_copy(1, step).wait_recv()
        low_face = summed(own_low + dot(stacked(got[0, step], elements), halo_picks[0]))
        high_face = summed(own_high + dot(stacked(got[1, step], elements), halo_picks[1]))
        state[:FACE, :] = following[:FACE] + edge * low_face
        state[FACE : ROWS - FACE, :] = following[FACE : ROWS - FACE]
        state[ROWS - FACE :, :] = following[ROWS - FACE :] + edge * high_face

        @pl.when(step < STEPS - 1)
        def _():
            fill(step + 1)
            for side in range(3):
                face_copy(side, step + 1).start()

        return carry

    lax.fori_loop(0, STEPS, advance, 0)

    fwd_out[...] = state[:NODES, :elements]
    adj_out[...] = state[:NODES, elements:]

    got_blocks[me] = blocks[me]

    def arrive(k, carry):
        block_arrival(k).wait_recv()
        return carry

    lax.fori_loop(1, devices, arrive, 0)
    arrived = got_blocks[...].reshape(devices * room, ROWS)
    cell = lax.broadcasted_iota(jnp.int32, (devices * room, P_DEV), 1) + 1
    chosen = jnp.where(arrived[:, NODES : NODES + 1] == cell.astype(F32), 1.0, 0.0)
    chosen = jnp.transpose(chosen).astype(BF16)
    arrived_high, arrived_low = split(arrived)
    grad = dot(chosen, arrived_high) + dot(chosen, arrived_low)
    grad_out[...] = grad[:, :NODES]

    def sent_off(k, carry):
        block_copy(k).wait_send()
        return carry

    lax.fori_loop(1, devices, sent_off, 0)
    for side in range(3):
        table_copy(side).wait_send()
        for step in range(STEPS):
            face_copy(side, step).wait_send()


def per_device(
    fwd_now,
    fwd_prev,
    adj_now,
    adj_prev,
    speed_sq,
    face_lists,
    send_low,
    send_high,
    send_radial,
    owner_dev,
    param_slot,
):
    operator, spread, factor, edge = constants()
    elements = fwd_now.shape[1]
    groups = lax.axis_size("group")
    layers = lax.axis_size("depth")
    devices = groups * layers
    capacity = elements // devices + elements // (2 * devices) + 2
    room = -(-capacity // 8) * 8
    both = 2 * elements

    def row(values):
        return jnp.pad(values, (0, elements - values.shape[0]), constant_values=-1)[None, :]

    table = jnp.concatenate(
        [
            face_lists,
            row(send_low),
            row(send_high),
            row(send_radial),
            owner_dev[:, 0][None, :],
            param_slot[None, :],
            jnp.zeros((TABLE - 11, elements), jnp.int32),
        ],
        axis=0,
    )
    vmem = pl.BlockSpec(memory_space=pltpu.VMEM)
    dma = pltpu.SemaphoreType.DMA
    return pl.pallas_call(
        functools.partial(kernel, (groups, layers, elements, capacity, room), edge),
        out_shape=(
            jax.ShapeDtypeStruct((NODES, elements), F32),
            jax.ShapeDtypeStruct((NODES, elements), F32),
            jax.ShapeDtypeStruct((P_DEV, NODES), F32),
        ),
        in_specs=[vmem] * 10,
        out_specs=(vmem, vmem, vmem),
        scratch_shapes=[
            pltpu.VMEM((ROWS, both), F32),
            pltpu.VMEM((ROWS, both), F32),
            pltpu.VMEM((ROWS, elements), F32),
            pltpu.VMEM((6, elements, elements), BF16),
            pltpu.VMEM((4, elements, elements), BF16),
            pltpu.VMEM((3, TABLE, elements), jnp.int32),
            pltpu.VMEM((3, STEPS, FACE, both), F32),
            pltpu.VMEM((3, STEPS, FACE, both), F32),
            pltpu.VMEM((devices, room, ROWS), F32),
            pltpu.VMEM((devices, room, ROWS), F32),
            dma((3,)),
            dma((3,)),
            dma((3, STEPS)),
            dma((3, STEPS)),
            dma((devices,)),
            dma((devices,)),
        ],
        compiler_params=pltpu.CompilerParams(
            collective_id=0, has_side_effects=True, vmem_limit_bytes=40 * 2**20
        ),
    )(
        fwd_now,
        fwd_prev,
        adj_now,
        adj_prev,
        speed_sq[None, :],
        table,
        owner_dev,
        jnp.asarray(operator),
        jnp.asarray(spread),
        jnp.asarray(factor),
    )


def solution(mesh):
    return jax.shard_map(
        per_device,
        mesh=mesh,
        in_specs=(
            P(None, ("group", "depth")),
            P(None, ("group", "depth")),
            P(None, ("group", "depth")),
            P(None, ("group", "depth")),
            P(("group", "depth")),
            P(None, ("group", "depth")),
            P(("group", "depth")),
            P(("group", "depth")),
            P(("group", "depth")),
            P(("group", "depth"), None),
            P(("group", "depth")),
        ),
        out_specs=(
            P(None, ("group", "depth")),
            P(None, ("group", "depth")),
            P(("group", "depth"), None),
        ),
        check_vma=False,
    )
```

```python
import functools
import math

import jax
import jax.numpy as jnp
import numpy as np
from jax import lax
from jax.experimental import pallas as pl
from jax.experimental.pallas import tpu as pltpu
from jax.sharding import PartitionSpec as P

NODES = 125
STEPS = 4
P_DEV = 128
ROWS = 128
FACE = 32

PENALTY = 40.0
DT_SQUARED = 0.001
KERNEL_SCALE = 0.05
MESH = pl.DeviceIdType.MESH
F32, BF16 = jnp.float32, jnp.bfloat16


def gll_tables():
    points = np.array([-1.0, -math.sqrt(3.0 / 7.0), 0.0, math.sqrt(3.0 / 7.0), 1.0])
    weights = np.array([0.1, 49.0 / 90.0, 32.0 / 45.0, 49.0 / 90.0, 0.1])
    barycentric = np.array(
        [np.prod([points[i] - points[m] for m in range(5) if m != i]) for i in range(5)]
    )
    derivative = np.zeros((5, 5))
    for i in range(5):
        for j in range(5):
            if i != j:
                derivative[i, j] = barycentric[i] / (barycentric[j] * (points[i] - points[j]))
            else:
                derivative[i, j] = sum((1.0 / (points[i] - points[m]) for m in range(5) if m != i))
    return (weights, derivative)


def padded(matrix, rows, columns):
    out = np.zeros((rows, columns))
    out[: matrix.shape[0], : matrix.shape[1]] = matrix
    return out


def constants():
    weights, derivative = gll_tables()
    one = np.eye(5)
    grads = [
        np.kron(derivative, np.kron(one, one)),
        np.kron(one, np.kron(derivative, one)),
        np.kron(one, np.kron(one, derivative)),
    ]
    cube = np.kron(weights, np.kron(weights, weights))
    stiff = sum(g.T @ (cube[:, None] * g) for g in grads) / cube[:, None]
    digits = [(n // 25, n // 5 % 5, n % 5) for n in range(NODES)]
    nodes_of = []
    for f in range(6):
        level = 0 if f % 2 == 0 else 4
        nodes_of.append([n for n in range(NODES) if digits[n][f // 2] == level])
    blocks = [padded(m, ROWS, ROWS) for m in grads + [stiff]]
    spread = np.zeros((ROWS, 4 * 2 * FACE))
    for f in range(2, 6):
        pick = np.zeros((FACE, ROWS))
        for a, n in enumerate(nodes_of[f]):
            pick[a, n] = 1.0
            spread[n, (f - 2) * 2 * FACE + a] = 1.0
            spread[n, (f - 2) * 2 * FACE + FACE + a] = 1.0
        blocks.append(pick)
    operator = np.concatenate(blocks, axis=0).astype(np.float32)
    bf = jnp.bfloat16
    high = operator.astype(bf)
    low = (operator - high.astype(np.float32)).astype(bf)
    operator = np.concatenate([high, high, low], axis=1)
    factor = np.zeros((2 * ROWS, 128), np.float32)
    faces = np.array([sum(n in set(nodes_of[f]) for f in range(6)) for n in range(NODES)])
    edge = DT_SQUARED * PENALTY / weights[0]
    factor[:NODES] = (2.0 - edge * faces)[:, None]
    factor[ROWS : ROWS + NODES] = (KERNEL_SCALE * cube)[:, None]
    return operator, spread.astype(bf), factor, edge


def split(values):
    high = values.astype(BF16)
    return high, (values - high.astype(F32)).astype(BF16)


def dot(a, b):
    return jnp.dot(a, b, preferred_element_type=F32)


def onehot(row, count, offset=0):
    places = lax.broadcasted_iota(jnp.int32, (count, row.shape[1]), 0) + offset
    return jnp.where(places == row, 1.0, 0.0).astype(BF16)


def filled(face):
    return jnp.concatenate([face, jnp.zeros((FACE - 25, face.shape[1]), F32)], axis=0)


def stacked(face):
    return jnp.concatenate(split(face), axis=0)


def kernel(
    sizes,
    edge,
    fwd_now,
    fwd_prev,
    adj_now,
    adj_prev,
    speed_in,
    lists_in,
    low_in,
    high_in,
    radial_in,
    owner_in,
    slot_in,
    operator_in,
    spread_in,
    factor_in,
    final,
    grad_out,
    state,
    raw,
    previous,
    following,
    slopes,
    total,
    speed,
    lists,
    owner,
    slot,
    operator,
    spread,
    factor,
    picks,
    halo_picks,
    peer_high,
    peer_low,
    peer_radial,
    sent,
    got,
    blocks,
    got_blocks,
    load_sem,
    table_send,
    table_recv,
    face_send,
    face_recv,
    block_send,
    block_recv,
):
    groups, layers, elements, capacity, room = sizes
    devices = groups * layers
    count = radial_in.shape[1]
    group, layer = lax.axis_index("group"), lax.axis_index("depth")
    me = group * layers + layer
    right = (lax.rem(group + 1, groups), layer)
    left = (lax.rem(group + groups - 1, groups), layer)
    across = (group, 1 - layer)
    partners = (right, left, across)

    loads = [
        pltpu.make_async_copy(source, target, load_sem.at[number])
        for number, (source, target) in enumerate(
            (
                (fwd_now, raw.at[0]),
                (adj_now, raw.at[1]),
                (operator_in, operator),
                (lists_in, lists),
                (owner_in, owner),
                (fwd_prev, raw.at[2]),
                (adj_prev, raw.at[3]),
                (spread_in, spread),
                (factor_in, factor),
                (speed_in, speed),
                (slot_in, slot),
            )
        )
    ]
    state[:, ROWS - 8 :, :] = jnp.zeros((2, 8, elements), F32)
    previous[:, ROWS - 8 :, :] = jnp.zeros((2, 8, elements), F32)
    total[...] = jnp.zeros_like(total)
    for load in loads:
        load.start()

    barrier = pltpu.get_barrier_semaphore()

    def at(number):
        return (number // layers, lax.rem(number, layers))

    def greet(k, carry):
        other = lax.rem(me + k, devices)
        pl.semaphore_signal(barrier, inc=1, device_id=at(other), device_id_type=MESH)
        return carry

    lax.fori_loop(1, devices, greet, 0)

    def table_copy(side):
        return pltpu.make_async_remote_copy(
            src_ref=(high_in, low_in, radial_in)[side],
            dst_ref=(peer_high, peer_low, peer_radial)[side],
            send_sem=table_send.at[side],
            recv_sem=table_recv.at[side],
            device_id=partners[side],
            device_id_type=MESH,
        )

    def face_copy(side, step, field):
        return pltpu.make_async_remote_copy(
            src_ref=sent.at[side, step, field],
            dst_ref=got.at[side, step, field],
            send_sem=face_send.at[side, step, field],
            recv_sem=face_recv.at[side, step, field],
            device_id=partners[side],
            device_id_type=MESH,
        )

    def block_copy(k, arriving=False):
        other = lax.rem(me + k, devices)
        place = other if arriving else me
        return pltpu.make_async_remote_copy(
            src_ref=blocks.at[other],
            dst_ref=got_blocks.at[place],
            send_sem=block_send.at[other],
            recv_sem=block_recv.at[place],
            device_id=at(other),
            device_id_type=MESH,
        )

    def fill_lateral(step, field):
        sent[0, step, field] = state[field, NODES - 25 : NODES, :]
        sent[1, step, field] = state[field, :25, :]

    def fill_radial(step, field):
        first = pl.multiple_of(4 * ROWS + 3 * FACE - FACE * layer, FACE)
        pick = operator[pl.ds(first, FACE), : 2 * ROWS]
        face = dot(pick, jnp.concatenate(split(state[field]), axis=0))
        sent[2, step, field] = face[:25]

    for field in range(2):
        loads[field].wait()
        state[field, :NODES, :] = raw[field]
        fill_lateral(0, field)
    pl.semaphore_wait(barrier, devices - 1)
    for field in range(2):
        face_copy(0, 0, field).start()
        face_copy(1, 0, field).start()
    for side in range(3):
        table_copy(side).start()
    loads[2].wait()
    for field in range(2):
        fill_radial(0, field)
        face_copy(2, 0, field).start()

    loads[3].wait()
    for f in range(6):
        picks[f] = onehot(lists[f : f + 1], elements)
    for load in loads[4:]:
        load.wait()
    for field in range(2):
        previous[field, :NODES, :] = raw[2 + field]

    def prepare(step, field):
        now = state[field]
        high, low = split(now)
        parts = dot(operator[...], jnp.concatenate([high, low, high], axis=0))
        if field == 0:
            slopes[...] = parts[: 3 * ROWS]
        else:
            product = total[...]
            for d in range(3):
                span = slice(d * ROWS, (d + 1) * ROWS)
                product = product + slopes[span] * parts[span]
            total[...] = product

            @pl.when(step == STEPS - 1)
            def _():
                share()

        face = [None, None] + [
            stacked(parts[4 * ROWS + f * FACE : 4 * ROWS + (f + 1) * FACE]) for f in range(4)
        ]
        found = [dot(face[3], picks[2]), dot(face[2], picks[3])]
        fourth, fifth = dot(face[5], picks[4]), dot(face[4], picks[5])
        face_copy(2, step, field).wait_recv()
        radial = stacked(filled(got[2, step, field]))
        found.append(fourth + dot(radial, halo_picks[2]))
        found.append(fifth + dot(radial, halo_picks[3]))
        penal = dot(spread[...], jnp.concatenate([one.astype(BF16) for one in found], axis=0))
        diagonal = jnp.concatenate([factor[:ROWS]] * (elements // 128), axis=1)
        after = diagonal * now - previous[field]
        after -= DT_SQUARED * speed[...] * parts[3 * ROWS : 4 * ROWS]
        following[field] = after + edge * penal
        previous[field] = now

    def lateral(side, step, field):
        found = dot(stacked(filled(sent[side, step, field])), picks[side])
        found += dot(stacked(filled(got[side, step, field])), halo_picks[side])
        return edge * (found[:FACE] + found[FACE:])

    def finish(step, field):
        face_copy(0, step, field).wait_recv()
        face_copy(1, step, field).wait_recv()
        state[field, :FACE, :] = following[field, :FACE, :] + lateral(0, step, field)
        raised = pltpu.roll(lateral(1, step, field), 4, 0)
        state[field, ROWS - FACE :, :] = following[field, ROWS - FACE :, :] + raised
        state[field, FACE : ROWS - FACE, :] = following[field, FACE : ROWS - FACE, :]

    def share():
        before_row = owner[...].astype(F32)
        square = jnp.broadcast_to(before_row, (elements, elements))
        before = (jnp.transpose(square) == square) & (
            lax.broadcasted_iota(jnp.int32, (elements, elements), 0)
            < lax.broadcasted_iota(jnp.int32, (elements, elements), 1)
        )
        position = jnp.sum(jnp.where(before, 1.0, 0.0), axis=0, keepdims=True).astype(jnp.int32)
        placer = onehot(owner[...] * room + position, devices * room)
        scale = jnp.concatenate([factor[ROWS:]] * (elements // 128), axis=1)
        block = scale * speed[...] * total[...]
        node = lax.broadcasted_iota(jnp.int32, (ROWS, elements), 0)
        block = jnp.where(node == NODES, (slot[...] + 1).astype(F32), block)
        block_high, block_low = split(block)
        last = (((1,), (1,)), ((), ()))
        placed = lax.dot_general(placer, block_high, last, preferred_element_type=F32)
        placed += lax.dot_general(placer, block_low, last, preferred_element_type=F32)
        blocks[...] = placed.reshape(devices, room, ROWS)

        def start(k, inner):
            block_copy(k).start()
            return inner

        lax.fori_loop(1, devices, start, 0)

    for side in range(3):
        table_copy(side).wait_recv()
    for place, (theirs, f, many) in enumerate(
        ((peer_high, 0, elements), (peer_low, 1, elements), (peer_radial, 4, count), (peer_radial, 5, count))
    ):
        mine = onehot(lists[f : f + 1], many, elements)
        halo_picks[place] = dot(onehot(theirs[...], elements), mine).astype(BF16)

    prepare(0, 0)
    prepare(0, 1)

    def advance(step, carry):
        for field in range(2):
            finish(step - 1, field)
            fill_lateral(step, field)
            face_copy(0, step, field).start()
            face_copy(1, step, field).start()
            fill_radial(step, field)
            face_copy(2, step, field).start()
            prepare(step, field)
        return carry

    lax.fori_loop(1, STEPS, advance, 0)
    for field in range(2):
        finish(STEPS - 1, field)
        final[field] = state[field, :NODES, :]

    got_blocks[me] = blocks[me]

    def arrive(k, carry):
        block_copy(k, True).wait_recv()
        return carry

    lax.fori_loop(1, devices, arrive, 0)
    arrived = got_blocks[...].reshape(devices * room, ROWS)
    cell = lax.broadcasted_iota(jnp.int32, (devices * room, P_DEV), 1) + 1
    chosen = jnp.where(arrived[:, NODES : NODES + 1] == cell.astype(F32), 1.0, 0.0)
    chosen = jnp.transpose(chosen).astype(BF16)
    arrived_high, arrived_low = split(arrived)
    grad = dot(chosen, arrived_high) + dot(chosen, arrived_low)
    grad_out[...] = grad[:, :NODES]

    def sent_off(k, carry):
        block_copy(k).wait_send()
        return carry

    lax.fori_loop(1, devices, sent_off, 0)
    for side in range(3):
        table_copy(side).wait_send()
        for step in range(STEPS):
            for field in range(2):
                face_copy(side, step, field).wait_send()


def deliver(final, grad, fwd_out, adj_out, grad_out, sem):
    copies = [
        pltpu.make_async_copy(final.at[0], fwd_out, sem.at[0]),
        pltpu.make_async_copy(final.at[1], adj_out, sem.at[1]),
        pltpu.make_async_copy(grad, grad_out, sem.at[2]),
    ]
    for copy in copies:
        copy.start()
    for copy in copies:
        copy.wait()


def per_device(
    fwd_now,
    fwd_prev,
    adj_now,
    adj_prev,
    speed_sq,
    face_lists,
    send_low,
    send_high,
    send_radial,
    owner_dev,
    param_slot,
):
    operator, spread, factor, edge = constants()
    elements = fwd_now.shape[1]
    groups = lax.axis_size("group")
    layers = lax.axis_size("depth")
    devices = groups * layers
    capacity = elements // devices + elements // (2 * devices) + 2
    room = -(-capacity // 8) * 8
    vmem = pl.BlockSpec(memory_space=pltpu.VMEM)
    hbm = pl.BlockSpec(memory_space=pltpu.HBM)
    dma = pltpu.SemaphoreType.DMA
    final, grad = pl.pallas_call(
        functools.partial(kernel, (groups, layers, elements, capacity, room), edge),
        out_shape=(
            jax.ShapeDtypeStruct((2, NODES, elements), F32),
            jax.ShapeDtypeStruct((P_DEV, NODES), F32),
        ),
        in_specs=[hbm] * 14,
        out_specs=(vmem, vmem),
        scratch_shapes=[
            pltpu.VMEM((2, ROWS, elements), F32),
            pltpu.VMEM((4, NODES, elements), F32),
            pltpu.VMEM((2, ROWS, elements), F32),
            pltpu.VMEM((2, ROWS, elements), F32),
            pltpu.VMEM((3 * ROWS, elements), F32),
            pltpu.VMEM((ROWS, elements), F32),
            pltpu.VMEM((1, elements), F32),
            pltpu.VMEM((6, elements), jnp.int32),
            pltpu.VMEM((1, elements), jnp.int32),
            pltpu.VMEM((1, elements), jnp.int32),
            pltpu.VMEM(operator.shape, BF16),
            pltpu.VMEM(spread.shape, BF16),
            pltpu.VMEM(factor.shape, F32),
            pltpu.VMEM((6, elements, elements), BF16),
            pltpu.VMEM((4, elements, elements), BF16),
            pltpu.VMEM((1, send_high.shape[0]), jnp.int32),
            pltpu.VMEM((1, send_low.shape[0]), jnp.int32),
            pltpu.VMEM((1, send_radial.shape[0]), jnp.int32),
            pltpu.VMEM((3, STEPS, 2, 25, elements), F32),
            pltpu.VMEM((3, STEPS, 2, 25, elements), F32),
            pltpu.VMEM((devices, room, ROWS), F32),
            pltpu.VMEM((devices, room, ROWS), F32),
            dma((11,)),
            dma((3,)),
            dma((3,)),
            dma((3, STEPS, 2)),
            dma((3, STEPS, 2)),
            dma((devices,)),
            dma((devices,)),
        ],
        compiler_params=pltpu.CompilerParams(
            collective_id=0, has_side_effects=True, vmem_limit_bytes=64 * 2**20 - 2**19
        ),
    )(
        fwd_now,
        fwd_prev,
        adj_now,
        adj_prev,
        speed_sq[None, :],
        face_lists,
        send_low[None, :],
        send_high[None, :],
        send_radial[None, :],
        owner_dev.reshape(1, elements),
        param_slot[None, :],
        jnp.asarray(operator),
        jnp.asarray(spread),
        jnp.asarray(factor),
    )
    return pl.pallas_call(
        deliver,
        out_shape=(
            jax.ShapeDtypeStruct((NODES, elements), F32),
            jax.ShapeDtypeStruct((NODES, elements), F32),
            jax.ShapeDtypeStruct((P_DEV, NODES), F32),
        ),
        in_specs=[hbm] * 2,
        out_specs=(hbm, hbm, hbm),
        scratch_shapes=[dma((3,))],
    )(final, grad)


def solution(mesh):
    return jax.shard_map(
        per_device,
        mesh=mesh,
        in_specs=(
            P(None, ("group", "depth")),
            P(None, ("group", "depth")),
            P(None, ("group", "depth")),
            P(None, ("group", "depth")),
            P(("group", "depth")),
            P(None, ("group", "depth")),
            P(("group", "depth")),
            P(("group", "depth")),
            P(("group", "depth")),
            P(("group", "depth"), None),
            P(("group", "depth")),
        ),
        out_specs=(
            P(None, ("group", "depth")),
            P(None, ("group", "depth")),
            P(("group", "depth"), None),
        ),
        check_vma=False,
    )
```

```python
import functools
import math

import jax
import jax.numpy as jnp
import numpy as np
from jax import lax
from jax.experimental import pallas as pl
from jax.experimental.pallas import tpu as pltpu
from jax.sharding import PartitionSpec as P

NODES = 125
STEPS = 4
P_DEV = 128
ROWS = 128
FACE = 32

PENALTY = 40.0
DT_SQUARED = 0.001
KERNEL_SCALE = 0.05
MESH = pl.DeviceIdType.MESH
F32, BF16 = jnp.float32, jnp.bfloat16


def gll_tables():
    points = np.array([-1.0, -math.sqrt(3.0 / 7.0), 0.0, math.sqrt(3.0 / 7.0), 1.0])
    weights = np.array([0.1, 49.0 / 90.0, 32.0 / 45.0, 49.0 / 90.0, 0.1])
    barycentric = np.array(
        [np.prod([points[i] - points[m] for m in range(5) if m != i]) for i in range(5)]
    )
    derivative = np.zeros((5, 5))
    for i in range(5):
        for j in range(5):
            if i != j:
                derivative[i, j] = barycentric[i] / (barycentric[j] * (points[i] - points[j]))
            else:
                derivative[i, j] = sum((1.0 / (points[i] - points[m]) for m in range(5) if m != i))
    return (weights, derivative)


def padded(matrix, rows, columns):
    out = np.zeros((rows, columns))
    out[: matrix.shape[0], : matrix.shape[1]] = matrix
    return out


def constants():
    weights, derivative = gll_tables()
    one = np.eye(5)
    grads = [
        np.kron(derivative, np.kron(one, one)),
        np.kron(one, np.kron(derivative, one)),
        np.kron(one, np.kron(one, derivative)),
    ]
    cube = np.kron(weights, np.kron(weights, weights))
    stiff = sum(g.T @ (cube[:, None] * g) for g in grads) / cube[:, None]
    digits = [(n // 25, n // 5 % 5, n % 5) for n in range(NODES)]
    nodes_of = []
    for f in range(6):
        level = 0 if f % 2 == 0 else 4
        nodes_of.append([n for n in range(NODES) if digits[n][f // 2] == level])
    blocks = [padded(m, ROWS, ROWS) for m in grads + [stiff]]
    spread = np.zeros((ROWS, 4 * 2 * FACE))
    for f in range(2, 6):
        pick = np.zeros((FACE, ROWS))
        for a, n in enumerate(nodes_of[f]):
            pick[a, n] = 1.0
            spread[n, (f - 2) * 2 * FACE + a] = 1.0
            spread[n, (f - 2) * 2 * FACE + FACE + a] = 1.0
        blocks.append(pick)
    operator = np.concatenate(blocks, axis=0).astype(np.float32)
    bf = jnp.bfloat16
    high = operator.astype(bf)
    low = (operator - high.astype(np.float32)).astype(bf)
    operator = np.concatenate([high, high, low], axis=1)
    factor = np.zeros((2 * ROWS, 128), np.float32)
    faces = np.array([sum(n in set(nodes_of[f]) for f in range(6)) for n in range(NODES)])
    edge = DT_SQUARED * PENALTY / weights[0]
    factor[:NODES] = (2.0 - edge * faces)[:, None]
    factor[ROWS : ROWS + NODES] = (KERNEL_SCALE * cube)[:, None]
    return operator, spread.astype(bf), factor, edge


def split(values):
    high = values.astype(BF16)
    return high, (values - high.astype(F32)).astype(BF16)


def dot(a, b):
    return jnp.dot(a, b, preferred_element_type=F32)


def onehot(row, count, offset=0):
    places = lax.broadcasted_iota(jnp.int32, (count, row.shape[1]), 0) + offset
    return jnp.where(places == row, 1.0, 0.0).astype(BF16)


def filled(face):
    return jnp.concatenate([face, jnp.zeros((FACE - 25, face.shape[1]), F32)], axis=0)


def stacked(face):
    return jnp.concatenate(split(face), axis=0)


def kernel(
    sizes,
    edge,
    fwd_now,
    fwd_prev,
    adj_now,
    adj_prev,
    speed_in,
    lists_in,
    low_in,
    high_in,
    radial_in,
    owner_in,
    slot_in,
    operator_in,
    spread_in,
    factor_in,
    final,
    grad_out,
    state,
    raw,
    previous,
    following,
    slopes,
    total,
    speed,
    lists,
    owner,
    slot,
    operator,
    spread,
    factor,
    picks,
    halo_picks,
    peer_high,
    peer_low,
    peer_radial,
    sent,
    got,
    blocks,
    got_blocks,
    load_sem,
    table_send,
    table_recv,
    face_send,
    face_recv,
    block_send,
    block_recv,
):
    groups, layers, elements, capacity, room = sizes
    devices = groups * layers
    count = radial_in.shape[1]
    group, layer = lax.axis_index("group"), lax.axis_index("depth")
    me = group * layers + layer
    right = (lax.rem(group + 1, groups), layer)
    left = (lax.rem(group + groups - 1, groups), layer)
    across = (group, 1 - layer)
    partners = (right, left, across)

    loads = [
        pltpu.make_async_copy(source, target, load_sem.at[number])
        for number, (source, target) in enumerate(
            (
                (fwd_now, raw.at[0]),
                (adj_now, raw.at[1]),
                (operator_in, operator),
                (lists_in, lists),
                (owner_in, owner),
                (fwd_prev, raw.at[2]),
                (adj_prev, raw.at[3]),
                (spread_in, spread),
                (factor_in, factor),
                (speed_in, speed),
                (slot_in, slot),
            )
        )
    ]
    state[:, ROWS - 8 :, :] = jnp.zeros((2, 8, elements), F32)
    previous[:, ROWS - 8 :, :] = jnp.zeros((2, 8, elements), F32)
    total[...] = jnp.zeros_like(total)
    for load in loads:
        load.start()

    barrier = pltpu.get_barrier_semaphore()

    def at(number):
        return (number // layers, lax.rem(number, layers))

    def greet(k, carry):
        other = lax.rem(me + k, devices)
        pl.semaphore_signal(barrier, inc=1, device_id=at(other), device_id_type=MESH)
        return carry

    lax.fori_loop(1, devices, greet, 0)

    def table_copy(side):
        return pltpu.make_async_remote_copy(
            src_ref=(high_in, low_in, radial_in)[side],
            dst_ref=(peer_high, peer_low, peer_radial)[side],
            send_sem=table_send.at[side],
            recv_sem=table_recv.at[side],
            device_id=partners[side],
            device_id_type=MESH,
        )

    def face_copy(side, step, field):
        return pltpu.make_async_remote_copy(
            src_ref=sent.at[side, step, field],
            dst_ref=got.at[side, step, field],
            send_sem=face_send.at[side, step, field],
            recv_sem=face_recv.at[side, step, field],
            device_id=partners[side],
            device_id_type=MESH,
        )

    def block_copy(k, arriving=False):
        other = lax.rem(me + k, devices)
        place = other if arriving else me
        return pltpu.make_async_remote_copy(
            src_ref=blocks.at[other],
            dst_ref=got_blocks.at[place],
            send_sem=block_send.at[other],
            recv_sem=block_recv.at[place],
            device_id=at(other),
            device_id_type=MESH,
        )

    def fill_lateral(step, field):
        sent[0, step, field] = state[field, NODES - 25 : NODES, :]
        sent[1, step, field] = state[field, :25, :]

    def fill_radial(step, field):
        first = pl.multiple_of(4 * ROWS + 3 * FACE - FACE * layer, FACE)
        pick = operator[pl.ds(first, FACE), : 2 * ROWS]
        face = dot(pick, jnp.concatenate(split(state[field]), axis=0))
        sent[2, step, field] = face[:25]

    for field in range(2):
        loads[field].wait()
        state[field, :NODES, :] = raw[field]
        fill_lateral(0, field)
    pl.semaphore_wait(barrier, devices - 1)
    for field in range(2):
        face_copy(0, 0, field).start()
        face_copy(1, 0, field).start()
    for side in range(3):
        table_copy(side).start()
    loads[2].wait()
    for field in range(2):
        fill_radial(0, field)
        face_copy(2, 0, field).start()

    loads[3].wait()
    for f in range(6):
        picks[f] = onehot(lists[f : f + 1], elements)
    for load in loads[4:]:
        load.wait()
    for field in range(2):
        previous[field, :NODES, :] = raw[2 + field]

    def prepare(step, field):
        now = state[field]
        high, low = split(now)
        parts = dot(operator[...], jnp.concatenate([high, low, high], axis=0))
        if field == 0:
            slopes[...] = parts[: 3 * ROWS]
        else:
            product = total[...]
            for d in range(3):
                span = slice(d * ROWS, (d + 1) * ROWS)
                product = product + slopes[span] * parts[span]
            total[...] = product

            @pl.when(step == STEPS - 1)
            def _():
                share()

        face = [None, None] + [
            stacked(parts[4 * ROWS + f * FACE : 4 * ROWS + (f + 1) * FACE]) for f in range(4)
        ]
        found = [dot(face[3], picks[2]), dot(face[2], picks[3])]
        fourth, fifth = dot(face[5], picks[4]), dot(face[4], picks[5])
        face_copy(2, step, field).wait_recv()
        radial = stacked(filled(got[2, step, field]))
        found.append(fourth + dot(radial, halo_picks[2]))
        found.append(fifth + dot(radial, halo_picks[3]))
        penal = dot(spread[...], jnp.concatenate([one.astype(BF16) for one in found], axis=0))
        diagonal = jnp.concatenate([factor[:ROWS]] * (elements // 128), axis=1)
        after = diagonal * now - previous[field]
        after -= DT_SQUARED * speed[...] * parts[3 * ROWS : 4 * ROWS]
        following[field] = after + edge * penal
        previous[field] = now

    def lateral(side, step, field):
        found = dot(stacked(filled(sent[side, step, field])), picks[side])
        found += dot(stacked(filled(got[side, step, field])), halo_picks[side])
        return edge * (found[:FACE] + found[FACE:])

    def finish(step, field):
        face_copy(0, step, field).wait_recv()
        face_copy(1, step, field).wait_recv()
        state[field, :FACE, :] = following[field, :FACE, :] + lateral(0, step, field)
        raised = pltpu.roll(lateral(1, step, field), 4, 0)
        state[field, ROWS - FACE :, :] = following[field, ROWS - FACE :, :] + raised
        state[field, FACE : ROWS - FACE, :] = following[field, FACE : ROWS - FACE, :]

    def share():
        before_row = owner[...].astype(F32)
        square = jnp.broadcast_to(before_row, (elements, elements))
        before = (jnp.transpose(square) == square) & (
            lax.broadcasted_iota(jnp.int32, (elements, elements), 0)
            < lax.broadcasted_iota(jnp.int32, (elements, elements), 1)
        )
        position = jnp.sum(jnp.where(before, 1.0, 0.0), axis=0, keepdims=True).astype(jnp.int32)
        placer = onehot(owner[...] * room + position, devices * room)
        scale = jnp.concatenate([factor[ROWS:]] * (elements // 128), axis=1)
        block = scale * speed[...] * total[...]
        node = lax.broadcasted_iota(jnp.int32, (ROWS, elements), 0)
        block = jnp.where(node == NODES, (slot[...] + 1).astype(F32), block)
        block_high, block_low = split(block)
        last = (((1,), (1,)), ((), ()))
        placed = lax.dot_general(placer, block_high, last, preferred_element_type=F32)
        placed += lax.dot_general(placer, block_low, last, preferred_element_type=F32)
        blocks[...] = placed.reshape(devices, room, ROWS)

        def start(k, inner):
            block_copy(k).start()
            return inner

        lax.fori_loop(1, devices, start, 0)

    for side in range(3):
        table_copy(side).wait_recv()
    for place, (theirs, f, many) in enumerate(
        ((peer_high, 0, elements), (peer_low, 1, elements), (peer_radial, 4, count), (peer_radial, 5, count))
    ):
        mine = onehot(lists[f : f + 1], many, elements)
        halo_picks[place] = dot(onehot(theirs[...], elements), mine).astype(BF16)

    prepare(0, 0)
    prepare(0, 1)

    def advance(step, carry):
        for field in range(2):
            finish(step - 1, field)
            fill_lateral(step, field)
            face_copy(0, step, field).start()
            face_copy(1, step, field).start()
            fill_radial(step, field)
            face_copy(2, step, field).start()
            prepare(step, field)
        return carry

    lax.fori_loop(1, STEPS, advance, 0)
    for field in range(2):
        finish(STEPS - 1, field)
        final[field] = state[field, :NODES, :]

    got_blocks[me] = blocks[me]

    def arrive(k, carry):
        block_copy(k, True).wait_recv()
        return carry

    lax.fori_loop(1, devices, arrive, 0)
    arrived = got_blocks[...].reshape(devices * room, ROWS)
    cell = lax.broadcasted_iota(jnp.int32, (devices * room, P_DEV), 1) + 1
    chosen = jnp.where(arrived[:, NODES : NODES + 1] == cell.astype(F32), 1.0, 0.0)
    chosen = jnp.transpose(chosen).astype(BF16)
    arrived_high, arrived_low = split(arrived)
    grad = dot(chosen, arrived_high) + dot(chosen, arrived_low)
    grad_out[...] = grad[:, :NODES]

    def sent_off(k, carry):
        block_copy(k).wait_send()
        return carry

    lax.fori_loop(1, devices, sent_off, 0)
    for side in range(3):
        table_copy(side).wait_send()
        for step in range(STEPS):
            for field in range(2):
                face_copy(side, step, field).wait_send()


def deliver(final, grad, fwd_out, adj_out, grad_out, sem):
    copies = [
        pltpu.make_async_copy(final.at[0], fwd_out, sem.at[0]),
        pltpu.make_async_copy(final.at[1], adj_out, sem.at[1]),
        pltpu.make_async_copy(grad, grad_out, sem.at[2]),
    ]
    for copy in copies:
        copy.start()
    for copy in copies:
        copy.wait()


def per_device(
    fwd_now,
    fwd_prev,
    adj_now,
    adj_prev,
    speed_sq,
    face_lists,
    send_low,
    send_high,
    send_radial,
    owner_dev,
    param_slot,
):
    operator, spread, factor, edge = constants()
    elements = fwd_now.shape[1]
    groups = lax.axis_size("group")
    layers = lax.axis_size("depth")
    devices = groups * layers
    capacity = elements // devices + elements // (2 * devices) + 2
    room = -(-capacity // 8) * 8
    vmem = pl.BlockSpec(memory_space=pltpu.VMEM)
    hbm = pl.BlockSpec(memory_space=pltpu.HBM)
    dma = pltpu.SemaphoreType.DMA
    final, grad = pl.pallas_call(
        functools.partial(kernel, (groups, layers, elements, capacity, room), edge),
        out_shape=(
            jax.ShapeDtypeStruct((2, NODES, elements), F32),
            jax.ShapeDtypeStruct((P_DEV, NODES), F32),
        ),
        in_specs=[hbm] * 14,
        out_specs=(vmem, vmem),
        scratch_shapes=[
            pltpu.VMEM((2, ROWS, elements), F32),
            pltpu.VMEM((4, NODES, elements), F32),
            pltpu.VMEM((2, ROWS, elements), F32),
            pltpu.VMEM((2, ROWS, elements), F32),
            pltpu.VMEM((3 * ROWS, elements), F32),
            pltpu.VMEM((ROWS, elements), F32),
            pltpu.VMEM((1, elements), F32),
            pltpu.VMEM((6, elements), jnp.int32),
            pltpu.VMEM((1, elements), jnp.int32),
            pltpu.VMEM((1, elements), jnp.int32),
            pltpu.VMEM(operator.shape, BF16),
            pltpu.VMEM(spread.shape, BF16),
            pltpu.VMEM(factor.shape, F32),
            pltpu.VMEM((6, elements, elements), BF16),
            pltpu.VMEM((4, elements, elements), BF16),
            pltpu.VMEM((1, send_high.shape[0]), jnp.int32),
            pltpu.VMEM((1, send_low.shape[0]), jnp.int32),
            pltpu.VMEM((1, send_radial.shape[0]), jnp.int32),
            pltpu.VMEM((3, STEPS, 2, 25, elements), F32),
            pltpu.VMEM((3, STEPS, 2, 25, elements), F32),
            pltpu.VMEM((devices, room, ROWS), F32),
            pltpu.VMEM((devices, room, ROWS), F32),
            dma((11,)),
            dma((3,)),
            dma((3,)),
            dma((3, STEPS, 2)),
            dma((3, STEPS, 2)),
            dma((devices,)),
            dma((devices,)),
        ],
        compiler_params=pltpu.CompilerParams(
            collective_id=0, has_side_effects=True, vmem_limit_bytes=64 * 2**20 - 2**19
        ),
    )(
        fwd_now,
        fwd_prev,
        adj_now,
        adj_prev,
        speed_sq[None, :],
        face_lists,
        send_low[None, :],
        send_high[None, :],
        send_radial[None, :],
        owner_dev.reshape(1, elements),
        param_slot[None, :],
        jnp.asarray(operator),
        jnp.asarray(spread),
        jnp.asarray(factor),
    )
    return pl.pallas_call(
        deliver,
        out_shape=(
            jax.ShapeDtypeStruct((NODES, elements), F32),
            jax.ShapeDtypeStruct((NODES, elements), F32),
            jax.ShapeDtypeStruct((P_DEV, NODES), F32),
        ),
        in_specs=[vmem] * 2,
        out_specs=(hbm, hbm, hbm),
        scratch_shapes=[dma((3,))],
    )(final, grad)


def solution(mesh):
    return jax.shard_map(
        per_device,
        mesh=mesh,
        in_specs=(
            P(None, ("group", "depth")),
            P(None, ("group", "depth")),
            P(None, ("group", "depth")),
            P(None, ("group", "depth")),
            P(("group", "depth")),
            P(None, ("group", "depth")),
            P(("group", "depth")),
            P(("group", "depth")),
            P(("group", "depth")),
            P(("group", "depth"), None),
            P(("group", "depth")),
        ),
        out_specs=(
            P(None, ("group", "depth")),
            P(None, ("group", "depth")),
            P(("group", "depth"), None),
        ),
        check_vma=False,
    )
```
